128 devices in a mesh: visit: 16 (over y_hi, x, core), strip: 8 (over y_lo, z).
Axes of the slice: x: 4, y: 4 (y_hi: 2, y_lo: 2; y = y_hi * 2 + y_lo), z: 4, core: 2. Of those that a mesh axis runs over, the one named last changes fastest.
Arguments:
- science: float32 [32, 512, 4096], P('visit', 'strip'), may hold values from -6 to 6
- template: float32 [512, 4096], P('strip', 'visit'), may hold values from -6 to 6
- gauss_widths: int32 [2], replicated, may hold values from 2 to 4
- coeff_orders: int32 [21], replicated, may hold values from 0 to 2
- coefficients: float32 [32, 21, 6], P('visit'), may hold values from -4 to 4
- back_coeffs: float32 [32, 6], P('visit'), may hold values from -3 to 3
- masks: int32 [32, 512, 4096], P('visit', 'strip'), may hold values from 0 to 4095
- decor_kernel: float32 [32, 11, 11], P('visit'), may hold values from -0.6 to 0.6
Outputs:
- decorrelated: float32 [32, 512, 4096], P('visit', 'strip')
The draws below stay inside these ranges and needn't reach their ends.
Inputs may be any that keep to these rules, and one draw needn't show every extreme that they name: `masks`: twelve mask planes a pixel.
All inputs are finite; a program needn't handle non-finite values.
Results may differ from the reference program's by a relative error of at most 0.0003.
Values sent between devices are 32-bit elements; how exact they have to be, the bound alone decides.
No kernel may reach another device: no remote copies, remote signals or barrier semaphores. Data moves between devices by JAX's collectives and lax.ppermute only.
A program may use at most 192 MiB of HBM per device.

```python
import jax
import jax.numpy as jnp
from jax import lax

COLS = 4096
KSIZE = 21
NBASIS = 21
NFILT = 8
NPOLY = 6
DKSIZE = 11
KHALF = 10
DHALF = 5
ROWS = 512
VISITS = 32


def set_ends(result, stream_key, low, high):
    shape = result.shape
    index_at = [jax.random.randint(jax.random.fold_in(stream_key, axis), (), 0, shape[axis]) for axis in range(len(shape))]
    result = result.at[tuple(index_at)].set(low)
    longest = shape.index(max(shape))
    index_at[longest] = (index_at[longest] + 1) % shape[longest]
    return result.at[tuple(index_at)].set(high)


def shard_levels(rng, shape, split, smallest, high):
    factor_of, own = 1.0, jax.random.fold_in(rng, 6)
    for dim, shards_of in split:
        heights = jnp.exp(jax.random.uniform(jax.random.fold_in(own, dim), (shards_of,), jnp.float32, smallest / len(split), high / len(split)))
        factor_of = factor_of * jnp.repeat(heights, shape[dim] // shards_of).reshape([-1 if axis == dim else 1 for axis in range(len(shape))])
    return factor_of


def scatter_about(own_key, extent, width, most, shards=(), held_as=jnp.bfloat16):
    loudness = shard_levels(own_key, extent, shards, -0.22, 0.18) if shards else 1.0
    values = jax.random.normal(own_key, extent, jnp.float32) * width * loudness
    return jnp.minimum(jnp.maximum(values, -most), most).astype(held_as)


def setup_inputs(seed: int = 0) -> dict:
    key_of = jax.random.split(jax.random.key(seed), 9)
    science = scatter_about(key_of[0], (VISITS, ROWS, COLS), 1.0, 6.0, ((0, 16), (1, 8)), jnp.float32)
    template = scatter_about(key_of[1], (ROWS, COLS), 1.0, 6.0, ((0, 8), (1, 16)), jnp.float32)
    gauss_widths = jax.random.randint(key_of[2], (2,), 2, 5).astype(jnp.int32)
    coeff_orders = set_ends(jax.random.randint(key_of[3], (NBASIS,), 0, 3), jax.random.fold_in(key_of[3], 1), 0, 2).astype(jnp.int32)
    coefficients = scatter_about(key_of[4], (VISITS, NBASIS, NPOLY), 1.0, 4.0, ((0, 16),), jnp.float32)
    back_coeffs = scatter_about(key_of[5], (VISITS, NPOLY), 0.5, 3.0, ((0, 16),), jnp.float32)
    masks = set_ends(jax.random.randint(key_of[6], (VISITS, ROWS, COLS), 0, 4096), jax.random.fold_in(key_of[6], 1), 0, 4095).astype(jnp.int32)
    decor_kernel = scatter_about(key_of[7], (VISITS, DKSIZE, DKSIZE), 0.1, 0.6, ((0, 16),), jnp.float32)
    return {"science": science, "template": template, "gauss_widths": gauss_widths, "coeff_orders": coeff_orders, "coefficients": coefficients, "back_coeffs": back_coeffs, "masks": masks, "decor_kernel": decor_kernel}


def kernel_table(gauss_widths):
    offsets = jnp.arange(KSIZE).astype(jnp.float32) - KHALF
    kernel_rows = []
    for family, degree in ((0, 4), (1, 2)):
        spread = 0.75 * gauss_widths[family].astype(jnp.float32)
        profile = jnp.exp(-offsets * offsets / (2.0 * spread * spread))
        profile = profile / jnp.sum(profile)
        scaled = offsets / spread
        for exponent in range(degree + 1):
            kernel_rows.append(scaled ** exponent * profile)
    return jnp.stack(kernel_rows)


def basis_pairs():
    basis_list = []
    for family_base, degree in ((0, 4), (5, 2)):
        for exponent in range(degree + 1):
            for second in range(degree + 1 - exponent):
                basis_list.append((family_base + exponent, family_base + second))
    return basis_list


def monomials(row_pos, total_rows, col_total):
    ynorm = (2.0 * row_pos.astype(jnp.float32) + 1.0) / total_rows - 1.0
    xnorm = (2.0 * jnp.arange(col_total).astype(jnp.float32) + 1.0) / col_total - 1.0
    ygrid = jnp.broadcast_to(ynorm[:, None], (row_pos.shape[0], col_total))
    xgrid = jnp.broadcast_to(xnorm[None, :], (row_pos.shape[0], col_total))
    return jnp.stack([jnp.ones_like(xgrid), xgrid, ygrid, xgrid * xgrid, xgrid * ygrid, ygrid * ygrid])


def reference(science, template, gauss_widths, coeff_orders, coefficients, back_coeffs, masks, decor_kernel):
    kernels = kernel_table(gauss_widths)
    padded = jnp.pad(template, KHALF)
    vertical = []
    for kernel_index in range(NFILT):
        running = jnp.zeros((ROWS, COLS + 2 * KHALF), jnp.float32)
        for tap_index in range(KSIZE):
            first_row = 2 * KHALF - tap_index
            running = running + kernels[kernel_index, tap_index] * padded[first_row:first_row + ROWS, :]
        vertical.append(running)
    images = []
    for row_kernel, col_kernel in basis_pairs():
        running = jnp.zeros((ROWS, COLS), jnp.float32)
        for tap_index in range(KSIZE):
            first_col = 2 * KHALF - tap_index
            running = running + kernels[col_kernel, tap_index] * vertical[row_kernel][:, first_col:first_col + COLS]
        images.append(running)
    images = jnp.stack(images)
    monomial_stack = monomials(jnp.arange(ROWS), ROWS, COLS)
    degrees = jnp.array([0, 1, 1, 2, 2, 2], jnp.int32)
    active = (degrees[None, :] <= coeff_orders[:, None]).astype(jnp.float32)
    effective = coefficients * active[None, :, :]

    def one_visit(items):
        visit_science, visit_coef, visit_back, visit_mask, visit_decor = items
        summed = jnp.einsum('kt,krc->trc', visit_coef, images, precision=lax.Precision.HIGHEST)
        model_image = jnp.sum(monomial_stack * (summed + visit_back[:, None, None]), axis=0)
        bad_pixel = jnp.bitwise_and(visit_mask, 7) == 7
        difference = jnp.where(bad_pixel, jnp.zeros_like(model_image), visit_science - model_image)
        padded_diff = jnp.pad(difference, DHALF)
        running = jnp.zeros((ROWS, COLS), jnp.float32)
        for row_tap in range(DKSIZE):
            for col_tap in range(DKSIZE):
                first_row = 2 * DHALF - row_tap
                first_col = 2 * DHALF - col_tap
                running = running + visit_decor[row_tap, col_tap] * padded_diff[first_row:first_row + ROWS, first_col:first_col + COLS]
        return running

    return lax.map(one_visit, (science, effective, back_coeffs, masks, decor_kernel))
```

```python
import jax
import jax.numpy as jnp
from jax import lax
from jax.experimental import pallas as pl
from jax.experimental.pallas import tpu as pltpu
from jax.sharding import PartitionSpec as P

KSIZE = 21
NBASIS = 21
NFILT = 8
NPOLY = 6
DKSIZE = 11
KHALF = 10
DHALF = 5
LANES = 128
CHUNK = 512
TROWS = 96
HALFROWS = 40
MROWS = 6 * HALFROWS
KWIN = 64
DROWS = 80
F32 = jnp.float32
BF16 = jnp.bfloat16


def basis_pairs():
    basis_list = []
    for family_base, degree in ((0, 4), (5, 2)):
        for exponent in range(degree + 1):
            for second in range(degree + 1 - exponent):
                basis_list.append((family_base + exponent, family_base + second))
    return basis_list


def kernel_table(gauss_widths):
    offsets = jnp.arange(KSIZE).astype(F32) - KHALF
    kernel_rows = []
    for family, degree in ((0, 4), (1, 2)):
        spread = 0.75 * gauss_widths[family].astype(F32)
        profile = jnp.exp(-offsets * offsets / (2.0 * spread * spread))
        profile = profile / jnp.sum(profile)
        scaled = offsets / spread
        for exponent in range(degree + 1):
            kernel_rows.append(scaled**exponent * profile)
    return jnp.stack(kernel_rows)


def high_part(x):
    return lax.reduce_precision(x, 8, 7)


def split(x):
    high = x.astype(BF16)
    return high, (x - high.astype(F32)).astype(BF16)


def strip_rows_norm(meta, half, strip_rows):
    rows = lax.broadcasted_iota(jnp.int32, (HALFROWS, LANES), 0) + (
        meta[0] * strip_rows - 8 + half * HALFROWS
    )
    return (2.0 * rows.astype(F32) + 1.0) / meta[2].astype(F32) - 1.0


def prepare(strip_rows, meta, filters, taps, decor_base, col_weights, row_weights, decor_weights):
    visits = decor_weights.shape[0]
    source = lax.broadcasted_iota(jnp.int32, (LANES, LANES), 0)
    target = lax.broadcasted_iota(jnp.int32, (LANES, LANES), 1)
    near = jnp.abs(target - source) <= KHALF
    for j in range(NFILT):
        lanes = slice(j * LANES, (j + 1) * LANES)
        flat = jnp.broadcast_to(filters[j][None, :], (LANES, LANES))
        ring = pltpu.roll(flat, 0, 1, stride=1, stride_axis=0)
        high = ring.astype(BF16).astype(F32)
        low = ring - high
        col_weights[:LANES, lanes] = jnp.where(near, high, 0.0).astype(BF16)
        col_weights[LANES : 2 * LANES, lanes] = jnp.where(near, high, 0.0).astype(BF16)
        col_weights[2 * LANES : 3 * LANES, lanes] = jnp.where(near, low, 0.0).astype(BF16)
        side_high = jnp.where(near, 0.0, high)
        side_low = jnp.where(near, 0.0, low)
        packed = side_high + pltpu.roll(side_high, 20, 0) + pltpu.roll(side_low, 40, 0)
        col_weights[3 * LANES :, lanes] = packed.astype(BF16)
    for half in range(2):
        yn = strip_rows_norm(meta, half, strip_rows)
        for tile in range(4):
            lanes = slice(tile * LANES, (tile + 1) * LANES)
            parts = []
            for s in range(visits):
                rolled = []
                for t in range(NPOLY):
                    flat = jnp.broadcast_to(taps[s * NPOLY + t, lanes][None, :], (HALFROWS, LANES))
                    rolled.append(pltpu.roll(flat, 8 * half, 1, stride=1, stride_axis=0))
                parts.append(rolled[0] + yn * (rolled[2] + yn * rolled[5]))
                parts.append(rolled[1] + yn * rolled[4])
                parts.append(rolled[3])
            high, low = split(jnp.concatenate(parts, axis=0))
            row_weights[half, :MROWS, lanes] = high
            row_weights[half, MROWS:, lanes] = low
    for s in range(visits):
        for b in range(DKSIZE):
            flat = jnp.broadcast_to(decor_base[s * DKSIZE + b][None, :], (strip_rows, 2 * LANES))
            turned = pltpu.roll(flat, 3, 1, stride=1, stride_axis=0)
            decor_weights[s, b * strip_rows : (b + 1) * strip_rows, :] = turned.astype(BF16)


def body(
    meta,
    back,
    own,
    other,
    col_weights,
    row_weights,
    decor_weights,
    science,
    masks,
    halo_up,
    halo_down,
    out,
    high_filtered,
    low_filtered,
    carry,
):
    step = pl.program_id(0)
    steps = pl.num_programs(0)
    core = meta[1]
    visits = science.shape[0]
    strip_rows = science.shape[1]

    @pl.when(step == 0)
    def clear():
        carry[...] = jnp.zeros_like(carry)

    mine, theirs = own[step], other[step]
    even = jnp.where(core == 0, mine, theirs)
    odd = jnp.where(core == 0, theirs, mine)
    before = jnp.maximum(step - 1, 0)
    after = jnp.minimum(step + 1, steps - 1)
    left = jnp.where(core == 0, other[before, :, LANES:], own[before, :, LANES:])
    left = jnp.where(step > 0, left, 0.0)
    right = jnp.where(core == 0, own[after, :, :LANES], other[after, :, :LANES])
    right = jnp.where(step < steps - 1, right, 0.0)
    blocks = [left, even[:, :LANES], even[:, LANES:], odd[:, :LANES], odd[:, LANES:], right]
    lane = lax.broadcasted_iota(jnp.int32, (TROWS, LANES), 1)
    stacked = []
    for b in range(4):
        high, low = split(blocks[b + 1])
        side = jnp.where(lane < KHALF, blocks[b + 2], jnp.where(lane >= LANES - KHALF, blocks[b], 0.0))
        side_high = side.astype(BF16).astype(F32)
        side_low = side - side_high
        packed = side_high + pltpu.roll(side_low, 20, 1) + pltpu.roll(side_high, 40, 1)
        stacked.append(jnp.concatenate([high, low, high, packed.astype(BF16)], axis=1))
    lhs = jnp.concatenate(stacked, axis=0)
    for pair in range(4):
        filtered = jnp.dot(
            lhs, col_weights[:, 256 * pair : 256 * (pair + 1)], preferred_element_type=F32
        )
        for inner in range(2):
            first = (2 * pair + inner) * TROWS
            for b in range(4):
                high, low = split(
                    filtered[TROWS * b : TROWS * (b + 1), LANES * inner : LANES * (inner + 1)]
                )
                high_filtered[first : first + TROWS, LANES * b : LANES * (b + 1)] = high
                low_filtered[first : first + TROWS, LANES * b : LANES * (b + 1)] = low

    columns = lax.broadcasted_iota(jnp.int32, (HALFROWS, CHUNK), 1) + step * CHUNK
    xn = (2.0 * columns.astype(F32) + 1.0) / float(steps * CHUNK) - 1.0
    models = [[None, None] for _ in range(visits)]
    for half in range(2):
        starts = [j * TROWS + 32 * half for j in range(NFILT)]
        rhs_high = jnp.concatenate([high_filtered[r : r + KWIN, :] for r in starts], axis=0)
        rhs_low = jnp.concatenate([low_filtered[r : r + KWIN, :] for r in starts], axis=0)
        wide = jnp.dot(row_weights[half], rhs_high, preferred_element_type=F32)
        rest = jnp.dot(row_weights[half, :MROWS, :], rhs_low, preferred_element_type=F32)
        summed = wide[:MROWS] + wide[MROWS:] + rest
        yn = strip_rows_norm(meta, half, strip_rows)[:, :1]
        for s in range(visits):
            base = s * 3 * HALFROWS
            back0 = back[s, 0] + yn * (back[s, 2] + yn * back[s, 5])
            back1 = back[s, 1] + yn * back[s, 4]
            g0 = summed[base : base + HALFROWS] + back0
            g1 = summed[base + HALFROWS : base + 2 * HALFROWS] + back1
            g2 = summed[base + 2 * HALFROWS : base + 3 * HALFROWS] + back[s, 3]
            models[s][half] = g0 + xn * (g1 + xn * g2)

    edge_lane = lax.broadcasted_iota(jnp.int32, (strip_rows, LANES), 1)
    start = pl.multiple_of(step * CHUNK, CHUNK)
    for s in range(visits):
        model = jnp.concatenate(models[s], axis=0)
        data = jnp.concatenate([halo_up[s, :8], science[s], halo_down[s, :8]], axis=0)
        fine = jnp.where(jnp.bitwise_and(masks[s], 7) == 7, 0.0, 1.0)
        good = jnp.concatenate([halo_up[s, 8:], fine, halo_down[s, 8:]], axis=0)
        diff = jnp.where(good > 0.5, data - model, 0.0)
        high, low = split(diff)
        rhs = jnp.concatenate([high, low, high, jnp.zeros((16, CHUNK), BF16)], axis=0)
        product = jnp.dot(decor_weights[s], rhs, preferred_element_type=F32)
        total = product[DHALF * strip_rows : (DHALF + 1) * strip_rows]
        to_right = jnp.zeros((strip_rows, LANES), F32)
        to_left = jnp.zeros((strip_rows, LANES), F32)
        for b in range(DKSIZE):
            shift = b - DHALF
            if shift == 0:
                continue
            turned = pltpu.roll(
                product[b * strip_rows : (b + 1) * strip_rows], shift % CHUNK, 1
            )
            if shift > 0:
                first = turned[:, :LANES]
                to_right = to_right + jnp.where(edge_lane < shift, first, 0.0)
                first = jnp.where(edge_lane < shift, 0.0, first)
                turned = jnp.concatenate([first, turned[:, LANES:]], axis=1)
            else:
                last = turned[:, CHUNK - LANES :]
                to_left = to_left + jnp.where(edge_lane >= LANES + shift, last, 0.0)
                last = jnp.where(edge_lane >= LANES + shift, 0.0, last)
                turned = jnp.concatenate([turned[:, : CHUNK - LANES], last], axis=1)
            total = total + turned
        out[s, :, pl.ds(start, LANES)] = total[:, :LANES] + carry[s]
        out[s, :, pl.ds(start + LANES, CHUNK - LANES)] = total[:, LANES:]
        carry[s] = to_right

        @pl.when(step > 0)
        def add_left():
            before_start = pl.multiple_of(start - LANES, LANES)
            out[s, :, pl.ds(before_start, LANES)] += to_left


def build_weights(visits, strip_rows, meta, filters, taps, decor_base):
    return pl.pallas_call(
        lambda *refs: prepare(strip_rows, *refs),
        out_shape=[
            jax.ShapeDtypeStruct((4 * LANES, NFILT * LANES), BF16),
            jax.ShapeDtypeStruct((2, 2 * MROWS, NFILT * KWIN), BF16),
            jax.ShapeDtypeStruct((visits, DKSIZE * strip_rows, 2 * LANES), BF16),
        ],
        in_specs=[pl.BlockSpec(memory_space=pltpu.SMEM)]
        + [pl.BlockSpec(memory_space=pltpu.VMEM)] * 3,
        compiler_params=pltpu.CompilerParams(vmem_limit_bytes=24 * 1024 * 1024),
        cost_estimate=pl.CostEstimate(flops=10**8, bytes_accessed=4 * 2**20, transcendentals=0),
    )(meta, filters, taps, decor_base)


def whole(array):
    return pl.BlockSpec(array.shape, lambda i: (0,) * len(array.shape))


def fused(
    meta,
    back,
    own,
    other,
    col_weights,
    row_weights,
    decor_weights,
    science,
    masks,
    halo_up,
    halo_down,
):
    visits, strip_rows, col_total = science.shape
    out = jax.ShapeDtypeStruct(science.shape, F32)
    return pl.pallas_call(
        body,
        grid=(col_total // CHUNK,),
        out_shape=out,
        in_specs=[
            pl.BlockSpec(memory_space=pltpu.SMEM),
            pl.BlockSpec(memory_space=pltpu.SMEM),
            whole(own),
            whole(other),
            whole(col_weights),
            whole(row_weights),
            whole(decor_weights),
            pl.BlockSpec((visits, strip_rows, CHUNK), lambda i: (0, 0, i)),
            pl.BlockSpec((visits, strip_rows, CHUNK), lambda i: (0, 0, i)),
            pl.BlockSpec((visits, 16, CHUNK), lambda i: (0, 0, i)),
            pl.BlockSpec((visits, 16, CHUNK), lambda i: (0, 0, i)),
        ],
        out_specs=whole(out),
        scratch_shapes=[
            pltpu.VMEM((NFILT * TROWS, CHUNK), BF16),
            pltpu.VMEM((NFILT * TROWS, CHUNK), BF16),
            pltpu.VMEM((visits, strip_rows, LANES), F32),
        ],
        compiler_params=pltpu.CompilerParams(
            dimension_semantics=("arbitrary",), vmem_limit_bytes=48 * 1024 * 1024
        ),
        cost_estimate=pl.CostEstimate(
            flops=14 * 10**9, bytes_accessed=10 * 2**20, transcendentals=0
        ),
    )(
        meta,
        back,
        own,
        other,
        col_weights,
        row_weights,
        decor_weights,
        science,
        masks,
        halo_up,
        halo_down,
    )


def shards(
    science, template, gauss_widths, coeff_orders, coefficients, back_coeffs, masks, decor_kernel
):
    visits, strip_rows, col_total = science.shape
    strips = lax.axis_size("strip")
    strip = lax.axis_index("strip")
    core = lax.axis_index("visit") % 2
    up = [(i, i + 1) for i in range(strips - 1)]
    down = [(i + 1, i) for i in range(strips - 1)]

    above = lax.ppermute(template[strip_rows - 16 :], "strip", up)
    below = lax.ppermute(template[:16], "strip", down)

    rimmed = jnp.concatenate([above, template, below], axis=0)
    rimmed, science_late, masks_late, gauss_widths, coefficients, decor_kernel = lax.optimization_barrier(
        (rimmed, science, masks, gauss_widths, coefficients, decor_kernel)
    )

    def edge(rows):
        good = jnp.where(jnp.bitwise_and(masks_late[:, rows], 7) == 7, 0.0, 1.0)
        return jnp.concatenate([science_late[:, rows], good], axis=1)

    halo_up = lax.ppermute(edge(slice(strip_rows - 8, strip_rows)), "strip", up)
    halo_down = lax.ppermute(edge(slice(0, 8)), "strip", down)

    kernels = kernel_table(gauss_widths)
    filters = jnp.roll(jnp.pad(kernels, ((0, 0), (0, LANES - KSIZE))), -KHALF, axis=1)
    degrees = jnp.array([0, 1, 1, 2, 2, 2], jnp.int32)
    active = (degrees[None, :] <= coeff_orders[:, None]).astype(F32)
    effective = coefficients * active[None, :, :]
    pairs = basis_pairs()
    row_onehot = jax.nn.one_hot(jnp.array([p[0] for p in pairs]), NFILT, dtype=F32)
    col_onehot = jax.nn.one_hot(jnp.array([p[1] for p in pairs]), NFILT, dtype=F32)
    by_row = jnp.einsum(
        "ki,id->kd", row_onehot, kernels, precision=lax.Precision.HIGHEST
    )
    placed = col_onehot[:, :, None] * by_row[:, None, ::-1]
    taps = jnp.einsum("skt,kjd->stjd", effective, placed, precision=lax.Precision.HIGHEST)
    taps = jnp.pad(taps, ((0, 0), (0, 0), (0, 0), (0, KWIN - KSIZE)))
    taps = taps.reshape(visits * NPOLY, NFILT * KWIN // LANES, LANES)
    taps = jnp.roll(taps, -2, axis=2).reshape(visits * NPOLY, NFILT * KWIN)

    flipped = jnp.swapaxes(decor_kernel[:, ::-1, :], 1, 2)
    decor_high = high_part(flipped)
    wide = ((0, 0), (0, 0), (0, DROWS - DKSIZE))
    decor_base = jnp.concatenate(
        [
            jnp.pad(decor_high, wide),
            jnp.pad(decor_high, wide),
            jnp.pad(flipped - decor_high, wide),
            jnp.zeros((visits, DKSIZE, 16), F32),
        ],
        axis=2,
    ).reshape(visits * DKSIZE, 2 * LANES)

    size = lax.axis_size("visit")
    groups = [[i for i in range(size) if i % 2 == c] for c in range(2)]
    chips = size // 2
    own = lax.all_to_all(
        jnp.broadcast_to(rimmed[None], (chips,) + rimmed.shape),
        "visit",
        0,
        0,
        axis_index_groups=groups,
    )
    other = lax.ppermute(own, "visit", [(i, i ^ 1) for i in range(size)])

    meta = jnp.stack([strip, core, strip_rows * strips]).astype(jnp.int32)
    weights = build_weights(visits, strip_rows, meta, filters, taps, decor_base)
    return fused(
        meta, back_coeffs, own, other, *weights, science, masks, halo_up, halo_down
    )


def solution(mesh):
    return jax.shard_map(
        shards,
        mesh=mesh,
        in_specs=(
            P("visit", "strip", None),
            P("strip", "visit"),
            P(),
            P(),
            P("visit", None, None),
            P("visit", None),
            P("visit", "strip", None),
            P("visit", None, None),
        ),
        out_specs=P("visit", "strip", None),
        check_vma=False,
    )
```

```python
import functools

import jax
import jax.numpy as jnp
from jax import lax
from jax.experimental import pallas as pl
from jax.experimental.pallas import tpu as pltpu
from jax.sharding import PartitionSpec as P

KSIZE = 21
NBASIS = 21
NFILT = 8
NPOLY = 6
DKSIZE = 11
KHALF = 10
DHALF = 5
LANES = 128
CHUNK = 512
SHIFTS = 4
GROUPS = 3
VMEM_LIMIT = 56 * 1024 * 1024
TROWS = 96
HALFROWS = 40
MROWS = 6 * HALFROWS
KWIN = 64
DROWS = 80
F32 = jnp.float32
BF16 = jnp.bfloat16


def basis_pairs():
    basis_list = []
    for family_base, degree in ((0, 4), (5, 2)):
        for exponent in range(degree + 1):
            for second in range(degree + 1 - exponent):
                basis_list.append((family_base + exponent, family_base + second))
    return basis_list


def split(x):
    high = x.astype(BF16)
    return high, (x - high.astype(F32)).astype(BF16)


def strip_rows_norm(meta, half, strip_rows):
    rows = lax.broadcasted_iota(jnp.int32, (HALFROWS, LANES), 0) + (
        meta[0] * strip_rows - 8 + half * HALFROWS
    )
    return (2.0 * rows.astype(F32) + 1.0) / meta[2].astype(F32) - 1.0


def family_filters(widths, position):
    offsets = lax.broadcasted_iota(jnp.int32, (1, LANES), 1) - LANES // 2
    rows = []
    for family, degree in ((0, 4), (1, 2)):
        spread = 0.75 * widths[family].astype(F32)

        def profile(at):
            real = at.astype(F32)
            return jnp.where(
                jnp.abs(at) <= KHALF, jnp.exp(-(real * real) / (2.0 * spread * spread)), 0.0
            )

        current = profile(position) / jnp.sum(profile(offsets), axis=1, keepdims=True)
        scaled = position.astype(F32) / spread
        for exponent in range(degree + 1):
            rows.append(current)
            current = current * scaled
    return rows


def prepare(
    strip_rows,
    meta,
    widths,
    orders,
    coefficients,
    decor_kernel,
    col_weights,
    row_weights,
    decor_weights,
):
    visits = decor_weights.shape[0]
    lane_row = lax.broadcasted_iota(jnp.int32, (1, LANES), 1)
    filters = family_filters(widths, jnp.where(lane_row < LANES // 2, lane_row, lane_row - LANES))
    place = jnp.where(lane_row >= LANES - 2, lane_row - LANES, lane_row) + 2
    odd_place = place >= KWIN
    inner = jnp.where(odd_place, place - KWIN, place)
    windows = family_filters(widths, KHALF - inner)
    degrees = (0, 1, 1, 2, 2, 2)
    taps = {}
    for s in range(visits):
        for t in range(NPOLY):
            sums = [None] * NFILT
            for k, (row_kernel, col_kernel) in enumerate(basis_pairs()):
                weight = jnp.where(orders[k] >= degrees[t], coefficients[s, k, t], 0.0)
                term = weight * windows[row_kernel]
                sums[col_kernel] = term if sums[col_kernel] is None else sums[col_kernel] + term
            for tile in range(NFILT // 2):
                taps[s, t, tile] = jnp.where(odd_place, sums[2 * tile + 1], sums[2 * tile])
    source = lax.broadcasted_iota(jnp.int32, (LANES, LANES), 0)
    target = lax.broadcasted_iota(jnp.int32, (LANES, LANES), 1)
    near = jnp.abs(target - source) <= KHALF
    for j in range(NFILT):
        lanes = slice(j * LANES, (j + 1) * LANES)
        flat = jnp.broadcast_to(filters[j], (LANES, LANES))
        ring = pltpu.roll(flat, 0, 1, stride=1, stride_axis=0)
        high = ring.astype(BF16).astype(F32)
        low = ring - high
        col_weights[:LANES, lanes] = jnp.where(near, high, 0.0).astype(BF16)
        col_weights[LANES : 2 * LANES, lanes] = jnp.where(near, high, 0.0).astype(BF16)
        col_weights[2 * LANES : 3 * LANES, lanes] = jnp.where(near, low, 0.0).astype(BF16)
        side_high = jnp.where(near, 0.0, high)
        side_low = jnp.where(near, 0.0, low)
        packed = side_high + pltpu.roll(side_high, 20, 0) + pltpu.roll(side_low, 40, 0)
        col_weights[3 * LANES :, lanes] = packed.astype(BF16)
    for half in range(2):
        yn = strip_rows_norm(meta, half, strip_rows)
        for tile in range(4):
            parts = []
            for s in range(visits):
                rolled = []
                for t in range(NPOLY):
                    flat = jnp.broadcast_to(taps[s, t, tile], (HALFROWS, LANES))
                    rolled.append(pltpu.roll(flat, 8 * half, 1, stride=1, stride_axis=0))
                parts.append(rolled[0] + yn * (rolled[2] + yn * rolled[5]))
                parts.append(rolled[1] + yn * rolled[4])
                parts.append(rolled[3])
            high, low = split(jnp.concatenate(parts, axis=0))
            lanes = slice(tile * LANES, (tile + 1) * LANES)
            row_weights[half, :MROWS, lanes] = high
            row_weights[half, MROWS:, lanes] = low
    for s in range(visits):
        for slot in range(SHIFTS * GROUPS):
            group, shift = slot // SHIFTS, slot % SHIFTS
            rows = slice(group * strip_rows, (group + 1) * strip_rows)
            lanes = slice(shift * 2 * LANES, (shift + 1) * 2 * LANES)
            if slot < DKSIZE:
                base = jnp.zeros((1, LANES), F32)
                for tap in range(DKSIZE):
                    base = jnp.where(lane_row == DKSIZE - 1 - tap, decor_kernel[s, tap, slot], base)
                high = base.astype(BF16).astype(F32)
                low = base - high
                wide = jnp.concatenate(
                    [high + pltpu.roll(high, DROWS, 1), pltpu.roll(low, 2 * DROWS - LANES, 1)], axis=1
                )
                flat = jnp.broadcast_to(wide, (strip_rows, 2 * LANES))
                turned = pltpu.roll(flat, 3, 1, stride=1, stride_axis=0).astype(BF16)
            else:
                turned = jnp.zeros((strip_rows, 2 * LANES), BF16)
            decor_weights[s, rows, lanes] = turned


def body(
    meta,
    back,
    own,
    other,
    col_weights,
    row_weights,
    decor_weights,
    science,
    masks,
    halo_up,
    halo_down,
    out,
    high_filtered,
    low_filtered,
    diffs,
    staged,
    sent,
):
    core = meta[1]
    visits, strip_rows, col_total = science.shape
    steps = col_total // CHUNK
    chips = CHUNK // 512
    blocks_here = 4 * chips
    diffs[:, :, col_total:] = jnp.zeros((visits, DROWS, LANES), F32)
    lane = lax.broadcasted_iota(jnp.int32, (TROWS, LANES), 1)
    edge_lane = lax.broadcasted_iota(jnp.int32, (strip_rows, LANES), 1)
    low_lanes, high_lanes = slice(0, LANES), slice(LANES, 2 * LANES)

    def strip_of(chip, odd, lanes):
        return jnp.where(core == odd, own[chip, :, lanes], other[chip, :, lanes])

    def differences(step):
        slot = step % 2
        first_chip = step * chips
        last_chip = first_chip + chips
        empty = jnp.zeros((TROWS, LANES), F32)
        blocks = [strip_of(first_chip - 1, 1, high_lanes) if step else empty]
        for chip in range(first_chip, last_chip):
            for odd in range(2):
                blocks.append(strip_of(chip, odd, low_lanes))
                blocks.append(strip_of(chip, odd, high_lanes))
        blocks.append(strip_of(last_chip, 0, low_lanes) if step < steps - 1 else empty)
        stacked = []
        for b in range(blocks_here):
            high, low = split(blocks[b + 1])
            side = jnp.where(
                lane < KHALF, blocks[b + 2], jnp.where(lane >= LANES - KHALF, blocks[b], 0.0)
            )
            side_high = side.astype(BF16).astype(F32)
            side_low = side - side_high
            packed = side_high + pltpu.roll(side_low, 20, 1) + pltpu.roll(side_high, 40, 1)
            stacked.append(jnp.concatenate([high, low, high, packed.astype(BF16)], axis=1))
        lhs = jnp.concatenate(stacked, axis=0)
        for pair in range(4):
            filtered = jnp.dot(
                lhs, col_weights[:, 256 * pair : 256 * (pair + 1)], preferred_element_type=F32
            )
            for inner in range(2):
                first = (2 * pair + inner) * TROWS
                for b in range(blocks_here):
                    high, low = split(
                        filtered[TROWS * b : TROWS * (b + 1), LANES * inner : LANES * (inner + 1)]
                    )
                    high_filtered[slot, first : first + TROWS, LANES * b : LANES * (b + 1)] = high
                    low_filtered[slot, first : first + TROWS, LANES * b : LANES * (b + 1)] = low

        columns = lax.broadcasted_iota(jnp.int32, (8, CHUNK), 1) + step * CHUNK
        xn = (2.0 * columns.astype(F32) + 1.0) / float(steps * CHUNK) - 1.0
        xn = jnp.concatenate([xn] * (HALFROWS // 8), axis=0)
        start = step * CHUNK
        span = slice(start, start + CHUNK)
        for half in range(2):
            starts = [j * TROWS + 32 * half for j in range(NFILT)]
            rhs_high = [high_filtered[slot, r : r + KWIN, :] for r in starts]
            rhs_low = [low_filtered[slot, r : r + KWIN, :] for r in starts]
            wide = jnp.dot(
                row_weights[half], jnp.concatenate(rhs_high, axis=0), preferred_element_type=F32
            )
            rest = jnp.dot(
                row_weights[half, :MROWS], jnp.concatenate(rhs_low, axis=0), preferred_element_type=F32
            )
            summed = wide[:MROWS] + wide[MROWS:] + rest
            yn = strip_rows_norm(meta, half, strip_rows)[:, :1]
            for s in range(visits):
                base = s * 3 * HALFROWS
                back0 = back[s, 0] + yn * (back[s, 2] + yn * back[s, 5])
                back1 = back[s, 1] + yn * back[s, 4]
                g0 = summed[base : base + HALFROWS] + back0
                g1 = summed[base + HALFROWS : base + 2 * HALFROWS] + back1
                g2 = summed[base + 2 * HALFROWS : base + 3 * HALFROWS] + back[s, 3]
                model = g0 + xn * (g1 + xn * g2)
                rows = slice(32 * half, 32 * half + 32)
                fine = jnp.where(jnp.bitwise_and(masks[s, rows, span], 7) == 7, 0.0, 1.0)
                data, good = science[s, rows, span], fine
                blank = jnp.zeros((8 - DHALF, CHUNK), F32)
                first = (step * visits + s) * 2 * DHALF
                halo = halo_down if half else halo_up
                halo_data = halo[first : first + DHALF]
                halo_good = halo[first + DHALF : first + 2 * DHALF]
                if half == 0:
                    data = jnp.concatenate([blank, halo_data, data], axis=0)
                    good = jnp.concatenate([blank, halo_good, good], axis=0)
                else:
                    data = jnp.concatenate([data, halo_data, blank], axis=0)
                    good = jnp.concatenate([good, halo_good, blank], axis=0)
                diffs[s, half * HALFROWS : (half + 1) * HALFROWS, span] = jnp.where(
                    good > 0.5, data - model, 0.0
                )

    def shifted_products(s, window, width):
        parts = []
        for shift in range(SHIFTS):
            turned = pltpu.roll(window, width + LANES - DHALF + shift, 1)[:, :width]
            high, low = split(turned)
            parts += [high, low, high, jnp.zeros((16, width), BF16)]
        return jnp.dot(
            decor_weights[s], jnp.concatenate(parts, axis=0), preferred_element_type=F32
        )

    def left_of_patch(s):
        window = jnp.concatenate([jnp.zeros((DROWS, LANES), F32), diffs[s, :, :LANES]], axis=1)
        product = shifted_products(s, window, LANES)
        start_carry = jnp.zeros((strip_rows, LANES), F32)
        for group in range(1, GROUPS):
            shift = SHIFTS * group
            turned = pltpu.roll(product[group * strip_rows : (group + 1) * strip_rows], shift, 1)
            start_carry = start_carry + jnp.where(edge_lane < shift, turned, 0.0)
        return start_carry

    def decorrelate(step, carries):
        start = step * CHUNK
        spilled = []
        for s in range(visits):
            product = shifted_products(s, diffs[s, :, start : start + CHUNK + LANES], CHUNK)
            total = product[:strip_rows]
            to_right = jnp.zeros((strip_rows, LANES), F32)
            for group in range(1, GROUPS):
                shift = SHIFTS * group
                turned = pltpu.roll(product[group * strip_rows : (group + 1) * strip_rows], shift, 1)
                first = turned[:, :LANES]
                to_right = to_right + jnp.where(edge_lane < shift, first, 0.0)
                first = jnp.where(edge_lane < shift, 0.0, first)
                total = total + jnp.concatenate([first, turned[:, LANES:]], axis=1)
            staged[s, :, start : start + LANES] = total[:, :LANES] + carries[s]
            staged[s, :, start + LANES : start + CHUNK] = total[:, LANES:]
            spilled.append(to_right)
        return spilled

    def send(step):
        span = pl.ds(step * CHUNK, CHUNK)
        return pltpu.make_async_copy(
            staged.at[:, :, span], out.at[:, :, span], sent.at[step]
        )

    for step in range(steps):
        differences(step)
    carries = [left_of_patch(s) for s in range(visits)]
    for step in range(steps):
        carries = decorrelate(step, carries)
        send(step).start()
    for step in range(steps):
        send(step).wait()


def pack_edges(science_top, science_bottom, masks_top, masks_bottom, edge_top, edge_bottom):
    for data, bits, edge, begin in (
        (science_top, masks_top, edge_top, 0),
        (science_bottom, masks_bottom, edge_bottom, 8 - DHALF),
    ):
        rows = slice(begin, begin + DHALF)
        for s in range(data.shape[0]):
            for chunk in range(data.shape[2] // CHUNK):
                span = slice(chunk * CHUNK, (chunk + 1) * CHUNK)
                first = (chunk * data.shape[0] + s) * 2 * DHALF
                edge[first : first + DHALF] = data[s, rows, span]
                edge[first + DHALF : first + 2 * DHALF] = jnp.where(
                    jnp.bitwise_and(bits[s, rows, span], 7) == 7, 0.0, 1.0
                )


def build_edges(science, masks):
    visits, strip_rows, col_total = science.shape
    block = (visits, 8, col_total)
    top = pl.BlockSpec(block, lambda i: (0, 0, 0))
    bottom = pl.BlockSpec(block, lambda i: (0, strip_rows // 8 - 1, 0))
    edge = jax.ShapeDtypeStruct((col_total // CHUNK * visits * 2 * DHALF, CHUNK), F32)
    return pl.pallas_call(
        pack_edges,
        grid=(1,),
        out_shape=[edge, edge],
        in_specs=[top, bottom, top, bottom],
        out_specs=[whole(edge), whole(edge)],
        compiler_params=pltpu.CompilerParams(vmem_limit_bytes=VMEM_LIMIT),
        cost_estimate=pl.CostEstimate(flops=10**6, bytes_accessed=2 * 2**20, transcendentals=0),
    )(science, science, masks, masks)


def build_weights(visits, strip_rows, meta, widths, orders, coefficients, decor_kernel):
    scalar = pl.BlockSpec(memory_space=pltpu.SMEM)
    return pl.pallas_call(
        functools.partial(prepare, strip_rows),
        out_shape=[
            jax.ShapeDtypeStruct((4 * LANES, NFILT * LANES), BF16),
            jax.ShapeDtypeStruct((2, 2 * MROWS, NFILT * KWIN), BF16),
            jax.ShapeDtypeStruct((visits, GROUPS * strip_rows, SHIFTS * 2 * LANES), BF16),
        ],
        in_specs=[scalar] * 5,
        compiler_params=pltpu.CompilerParams(vmem_limit_bytes=VMEM_LIMIT),
        cost_estimate=pl.CostEstimate(flops=10**9, bytes_accessed=8 * 2**20, transcendentals=0),
    )(meta, widths, orders, coefficients, decor_kernel)


def whole(array):
    return pl.BlockSpec(array.shape, lambda i: (0,) * len(array.shape))


def fused(meta, back, templates, weights, science, masks, halo_up, halo_down):
    visits, strip_rows, col_total = science.shape
    return pl.pallas_call(
        body,
        out_shape=jax.ShapeDtypeStruct(science.shape, F32),
        in_specs=[pl.BlockSpec(memory_space=pltpu.SMEM)] * 2
        + [pl.BlockSpec(memory_space=pltpu.VMEM)] * 9,
        out_specs=pl.BlockSpec(memory_space=pl.ANY),
        scratch_shapes=[
            pltpu.VMEM((2, NFILT * TROWS, CHUNK), BF16),
            pltpu.VMEM((2, NFILT * TROWS, CHUNK), BF16),
            pltpu.VMEM((visits, DROWS, col_total + LANES), F32),
            pltpu.VMEM((visits, strip_rows, col_total), F32),
            pltpu.SemaphoreType.DMA((col_total // CHUNK,)),
        ],
        compiler_params=pltpu.CompilerParams(vmem_limit_bytes=20 * 1024 * 1024),
        cost_estimate=pl.CostEstimate(
            flops=14 * 10**9, bytes_accessed=10 * 2**20, transcendentals=0
        ),
    )(meta, back, *templates, *weights, science, masks, halo_up, halo_down)


def shards(
    science, template, gauss_widths, coeff_orders, coefficients, back_coeffs, masks, decor_kernel
):
    visits, strip_rows, col_total = science.shape
    strips = lax.axis_size("strip")
    strip = lax.axis_index("strip")
    core = lax.axis_index("visit") % 2
    up = [(i, i + 1) for i in range(strips - 1)]
    down = [(i + 1, i) for i in range(strips - 1)]

    size = lax.axis_size("visit")
    groups = [[i for i in range(size) if i % 2 == c] for c in range(2)]
    chips = size // 2
    above = lax.ppermute(template[strip_rows - 16 :], "strip", up)
    below = lax.ppermute(template[:16], "strip", down)
    edge_top, edge_bottom = build_edges(science, masks)
    above, below, edge_top, edge_bottom = lax.optimization_barrier(
        (above, below, edge_top, edge_bottom)
    )
    rimmed = jnp.concatenate([above, template, below], axis=0)
    copies = jnp.broadcast_to(rimmed[None], (chips,) + rimmed.shape)
    small = (copies, edge_top, edge_bottom, gauss_widths, coeff_orders, coefficients, decor_kernel)
    copies, edge_top, edge_bottom, *parameters = lax.optimization_barrier(small)
    own = lax.all_to_all(copies, "visit", 0, 0, axis_index_groups=groups)
    halo_up = lax.ppermute(edge_bottom, "strip", up)
    halo_down = lax.ppermute(edge_top, "strip", down)
    meta = jnp.stack([strip, core, strip_rows * strips]).astype(jnp.int32)
    weights = build_weights(visits, strip_rows, meta, *parameters)
    own, weights, halo_up, halo_down = lax.optimization_barrier((own, weights, halo_up, halo_down))
    other = lax.ppermute(own, "visit", [(i, i ^ 1) for i in range(size)])
    return fused(meta, back_coeffs, (own, other), weights, science, masks, halo_up, halo_down)


def solution(mesh):
    return jax.shard_map(
        shards,
        mesh=mesh,
        in_specs=(
            P("visit", "strip", None),
            P("strip", "visit"),
            P(),
            P(),
            P("visit", None, None),
            P("visit", None),
            P("visit", "strip", None),
            P("visit", None, None),
        ),
        out_specs=P("visit", "strip", None),
        check_vma=False,
    )
```

```python
import functools

import jax
import jax.numpy as jnp
from jax import lax
from jax.experimental import pallas as pl
from jax.experimental.pallas import tpu as pltpu
from jax.sharding import PartitionSpec as P

KSIZE = 21
NBASIS = 21
NFILT = 8
NPOLY = 6
DKSIZE = 11
KHALF = 10
DHALF = 5
LANES = 128
CHUNK = 512
SHIFTS = 4
GROUPS = 3
VMEM_LIMIT = 56 * 1024 * 1024
TROWS = 96
HALFROWS = 40
MROWS = 6 * HALFROWS
KWIN = 64
DROWS = 80
F32 = jnp.float32
BF16 = jnp.bfloat16


def basis_pairs():
    basis_list = []
    for family_base, degree in ((0, 4), (5, 2)):
        for exponent in range(degree + 1):
            for second in range(degree + 1 - exponent):
                basis_list.append((family_base + exponent, family_base + second))
    return basis_list


def split(x):
    high = x.astype(BF16)
    return high, (x - high.astype(F32)).astype(BF16)


def strip_rows_norm(meta, half, strip_rows):
    rows = lax.broadcasted_iota(jnp.int32, (HALFROWS, LANES), 0) + (
        meta[0] * strip_rows - 8 + half * HALFROWS
    )
    return (2.0 * rows.astype(F32) + 1.0) / meta[2].astype(F32) - 1.0


def family_filters(widths, position):
    offsets = lax.broadcasted_iota(jnp.int32, (1, LANES), 1) - LANES // 2
    rows = []
    for family, degree in ((0, 4), (1, 2)):
        spread = 0.75 * widths[family].astype(F32)

        def profile(at):
            real = at.astype(F32)
            return jnp.where(
                jnp.abs(at) <= KHALF, jnp.exp(-(real * real) / (2.0 * spread * spread)), 0.0
            )

        current = profile(position) / jnp.sum(profile(offsets), axis=1, keepdims=True)
        scaled = position.astype(F32) / spread
        for exponent in range(degree + 1):
            rows.append(current)
            current = current * scaled
    return rows


def prepare(
    strip_rows,
    meta,
    widths,
    orders,
    coefficients,
    decor_kernel,
    col_weights,
    row_weights,
    decor_weights,
    token,
):
    token[...] = jnp.zeros_like(token)
    visits = decor_weights.shape[0]
    lane_row = lax.broadcasted_iota(jnp.int32, (1, LANES), 1)
    filters = family_filters(widths, jnp.where(lane_row < LANES // 2, lane_row, lane_row - LANES))
    place = jnp.where(lane_row >= LANES - 2, lane_row - LANES, lane_row) + 2
    odd_place = place >= KWIN
    inner = jnp.where(odd_place, place - KWIN, place)
    windows = family_filters(widths, KHALF - inner)
    degrees = (0, 1, 1, 2, 2, 2)
    taps = {}
    for s in range(visits):
        for t in range(NPOLY):
            sums = [None] * NFILT
            for k, (row_kernel, col_kernel) in enumerate(basis_pairs()):
                weight = jnp.where(orders[k] >= degrees[t], coefficients[s, k, t], 0.0)
                term = weight * windows[row_kernel]
                sums[col_kernel] = term if sums[col_kernel] is None else sums[col_kernel] + term
            for tile in range(NFILT // 2):
                taps[s, t, tile] = jnp.where(odd_place, sums[2 * tile + 1], sums[2 * tile])
    source = lax.broadcasted_iota(jnp.int32, (LANES, LANES), 0)
    target = lax.broadcasted_iota(jnp.int32, (LANES, LANES), 1)
    near = jnp.abs(target - source) <= KHALF
    for j in range(NFILT):
        lanes = slice(j * LANES, (j + 1) * LANES)
        flat = jnp.broadcast_to(filters[j], (LANES, LANES))
        ring = pltpu.roll(flat, 0, 1, stride=1, stride_axis=0)
        high = ring.astype(BF16).astype(F32)
        low = ring - high
        col_weights[:LANES, lanes] = jnp.where(near, high, 0.0).astype(BF16)
        col_weights[LANES : 2 * LANES, lanes] = jnp.where(near, high, 0.0).astype(BF16)
        col_weights[2 * LANES : 3 * LANES, lanes] = jnp.where(near, low, 0.0).astype(BF16)
        side_high = jnp.where(near, 0.0, high)
        side_low = jnp.where(near, 0.0, low)
        packed = side_high + pltpu.roll(side_high, 20, 0) + pltpu.roll(side_low, 40, 0)
        col_weights[3 * LANES :, lanes] = packed.astype(BF16)
    for half in range(2):
        yn = strip_rows_norm(meta, half, strip_rows)
        for tile in range(4):
            parts = []
            for s in range(visits):
                rolled = []
                for t in range(NPOLY):
                    flat = jnp.broadcast_to(taps[s, t, tile], (HALFROWS, LANES))
                    rolled.append(pltpu.roll(flat, 8 * half, 1, stride=1, stride_axis=0))
                parts.append(rolled[0] + yn * (rolled[2] + yn * rolled[5]))
                parts.append(rolled[1] + yn * rolled[4])
                parts.append(rolled[3])
            high, low = split(jnp.concatenate(parts, axis=0))
            lanes = slice(tile * LANES, (tile + 1) * LANES)
            row_weights[half, :MROWS, lanes] = high
            row_weights[half, MROWS:, lanes] = low
    for s in range(visits):
        for slot in range(SHIFTS * GROUPS):
            group, shift = slot // SHIFTS, slot % SHIFTS
            rows = slice(group * strip_rows, (group + 1) * strip_rows)
            lanes = slice(shift * 2 * LANES, (shift + 1) * 2 * LANES)
            if slot < DKSIZE:
                base = jnp.zeros((1, LANES), F32)
                for tap in range(DKSIZE):
                    base = jnp.where(lane_row == DKSIZE - 1 - tap, decor_kernel[s, tap, slot], base)
                high = base.astype(BF16).astype(F32)
                low = base - high
                wide = jnp.concatenate(
                    [high + pltpu.roll(high, DROWS, 1), pltpu.roll(low, 2 * DROWS - LANES, 1)], axis=1
                )
                flat = jnp.broadcast_to(wide, (strip_rows, 2 * LANES))
                turned = pltpu.roll(flat, 3, 1, stride=1, stride_axis=0).astype(BF16)
            else:
                turned = jnp.zeros((strip_rows, 2 * LANES), BF16)
            decor_weights[s, rows, lanes] = turned


def body(
    meta,
    back,
    token,
    own,
    other,
    col_source,
    row_source,
    decor_source,
    science,
    masks_source,
    halo_up,
    halo_down,
    out,
    high_filtered,
    low_filtered,
    diffs,
    staged,
    col_weights,
    row_weights,
    decor_weights,
    masks,
    sent,
    arrived,
):
    fetches = [
        pltpu.make_async_copy(source, copy, arrived.at[index])
        for index, (source, copy) in enumerate(
            (
                (col_source, col_weights),
                (row_source, row_weights),
                (masks_source, masks),
                (decor_source, decor_weights),
            )
        )
    ]
    fetches[0].start()
    fetches[1].start()
    core = meta[1]
    visits, strip_rows, col_total = science.shape
    steps = col_total // CHUNK
    chips = CHUNK // 512
    blocks_here = 4 * chips
    diffs[:, :, col_total:] = jnp.zeros((visits, DROWS, LANES), F32)
    lane = lax.broadcasted_iota(jnp.int32, (TROWS, LANES), 1)
    edge_lane = lax.broadcasted_iota(jnp.int32, (strip_rows, LANES), 1)
    low_lanes, high_lanes = slice(0, LANES), slice(LANES, 2 * LANES)

    def strip_of(chip, odd, lanes):
        return jnp.where(core == odd, own[chip, :, lanes], other[chip, :, lanes])

    def differences(step):
        slot = step % 2
        first_chip = step * chips
        last_chip = first_chip + chips
        empty = jnp.zeros((TROWS, LANES), F32)
        blocks = [strip_of(first_chip - 1, 1, high_lanes) if step else empty]
        for chip in range(first_chip, last_chip):
            for odd in range(2):
                blocks.append(strip_of(chip, odd, low_lanes))
                blocks.append(strip_of(chip, odd, high_lanes))
        blocks.append(strip_of(last_chip, 0, low_lanes) if step < steps - 1 else empty)
        stacked = []
        for b in range(blocks_here):
            high, low = split(blocks[b + 1])
            side = jnp.where(
                lane < KHALF, blocks[b + 2], jnp.where(lane >= LANES - KHALF, blocks[b], 0.0)
            )
            side_high = side.astype(BF16).astype(F32)
            side_low = side - side_high
            packed = side_high + pltpu.roll(side_low, 20, 1) + pltpu.roll(side_high, 40, 1)
            stacked.append(jnp.concatenate([high, low, high, packed.astype(BF16)], axis=1))
        lhs = jnp.concatenate(stacked, axis=0)
        for pair in range(4):
            filtered = jnp.dot(
                lhs, col_weights[:, 256 * pair : 256 * (pair + 1)], preferred_element_type=F32
            )
            for inner in range(2):
                first = (2 * pair + inner) * TROWS
                for b in range(blocks_here):
                    high, low = split(
                        filtered[TROWS * b : TROWS * (b + 1), LANES * inner : LANES * (inner + 1)]
                    )
                    high_filtered[slot, first : first + TROWS, LANES * b : LANES * (b + 1)] = high
                    low_filtered[slot, first : first + TROWS, LANES * b : LANES * (b + 1)] = low

        if step == 0:
            fetches[1].wait()
        columns = lax.broadcasted_iota(jnp.int32, (8, CHUNK), 1) + step * CHUNK
        xn = (2.0 * columns.astype(F32) + 1.0) / float(steps * CHUNK) - 1.0
        xn = jnp.concatenate([xn] * (HALFROWS // 8), axis=0)
        start = step * CHUNK
        span = slice(start, start + CHUNK)
        for half in range(2):
            starts = [j * TROWS + 32 * half for j in range(NFILT)]
            rhs_high = [high_filtered[slot, r : r + KWIN, :] for r in starts]
            rhs_low = [low_filtered[slot, r : r + KWIN, :] for r in starts]
            wide = jnp.dot(
                row_weights[half], jnp.concatenate(rhs_high, axis=0), preferred_element_type=F32
            )
            rest = jnp.dot(
                row_weights[half, :MROWS], jnp.concatenate(rhs_low, axis=0), preferred_element_type=F32
            )
            summed = wide[:MROWS] + wide[MROWS:] + rest
            if step == 0 and half == 0:
                fetches[2].wait()
            yn = strip_rows_norm(meta, half, strip_rows)[:, :1]
            for s in range(visits):
                base = s * 3 * HALFROWS
                back0 = back[s, 0] + yn * (back[s, 2] + yn * back[s, 5])
                back1 = back[s, 1] + yn * back[s, 4]
                g0 = summed[base : base + HALFROWS] + back0
                g1 = summed[base + HALFROWS : base + 2 * HALFROWS] + back1
                g2 = summed[base + 2 * HALFROWS : base + 3 * HALFROWS] + back[s, 3]
                model = g0 + xn * (g1 + xn * g2)
                rows = slice(32 * half, 32 * half + 32)
                fine = jnp.where(jnp.bitwise_and(masks[s, rows, span], 7) == 7, 0.0, 1.0)
                data, good = science[s, rows, span], fine
                blank = jnp.zeros((8 - DHALF, CHUNK), F32)
                first = (step * visits + s) * 2 * DHALF
                halo = halo_down if half else halo_up
                halo_data = halo[first : first + DHALF]
                halo_good = halo[first + DHALF : first + 2 * DHALF]
                if half == 0:
                    data = jnp.concatenate([blank, halo_data, data], axis=0)
                    good = jnp.concatenate([blank, halo_good, good], axis=0)
                else:
                    data = jnp.concatenate([data, halo_data, blank], axis=0)
                    good = jnp.concatenate([good, halo_good, blank], axis=0)
                diffs[s, half * HALFROWS : (half + 1) * HALFROWS, span] = jnp.where(
                    good > 0.5, data - model, 0.0
                )

    def shifted_products(s, window, width):
        parts = []
        for shift in range(SHIFTS):
            turned = pltpu.roll(window, width + LANES - DHALF + shift, 1)[:, :width]
            high, low = split(turned)
            parts += [high, low, high, jnp.zeros((16, width), BF16)]
        return jnp.dot(
            decor_weights[s], jnp.concatenate(parts, axis=0), preferred_element_type=F32
        )

    def left_of_patch(s):
        window = jnp.concatenate([jnp.zeros((DROWS, LANES), F32), diffs[s, :, :LANES]], axis=1)
        product = shifted_products(s, window, LANES)
        start_carry = jnp.zeros((strip_rows, LANES), F32)
        for group in range(1, GROUPS):
            shift = SHIFTS * group
            turned = pltpu.roll(product[group * strip_rows : (group + 1) * strip_rows], shift, 1)
            start_carry = start_carry + jnp.where(edge_lane < shift, turned, 0.0)
        return start_carry

    def decorrelate(step, carries):
        start = step * CHUNK
        spilled = []
        for s in range(visits):
            product = shifted_products(s, diffs[s, :, start : start + CHUNK + LANES], CHUNK)
            total = product[:strip_rows]
            to_right = jnp.zeros((strip_rows, LANES), F32)
            for group in range(1, GROUPS):
                shift = SHIFTS * group
                turned = pltpu.roll(product[group * strip_rows : (group + 1) * strip_rows], shift, 1)
                first = turned[:, :LANES]
                to_right = to_right + jnp.where(edge_lane < shift, first, 0.0)
                first = jnp.where(edge_lane < shift, 0.0, first)
                total = total + jnp.concatenate([first, turned[:, LANES:]], axis=1)
            staged[s, :, start : start + LANES] = total[:, :LANES] + carries[s]
            staged[s, :, start + LANES : start + CHUNK] = total[:, LANES:]
            spilled.append(to_right)
        return spilled

    def send(step):
        span = pl.ds(step * CHUNK, CHUNK)
        return pltpu.make_async_copy(
            staged.at[:, :, span], out.at[:, :, span], sent.at[step]
        )

    fetches[0].wait()
    fetches[2].start()
    fetches[3].start()
    for step in range(steps):
        differences(step)
    fetches[3].wait()
    carries = [left_of_patch(s) for s in range(visits)]
    for step in range(steps):
        carries = decorrelate(step, carries)
        send(step).start()
    for step in range(steps):
        send(step).wait()


def pack_edges(science_top, science_bottom, masks_top, masks_bottom, edge_top, edge_bottom):
    for data, bits, edge, begin in (
        (science_top, masks_top, edge_top, 0),
        (science_bottom, masks_bottom, edge_bottom, 8 - DHALF),
    ):
        rows = slice(begin, begin + DHALF)
        for s in range(data.shape[0]):
            for chunk in range(data.shape[2] // CHUNK):
                span = slice(chunk * CHUNK, (chunk + 1) * CHUNK)
                first = (chunk * data.shape[0] + s) * 2 * DHALF
                edge[first : first + DHALF] = data[s, rows, span]
                edge[first + DHALF : first + 2 * DHALF] = jnp.where(
                    jnp.bitwise_and(bits[s, rows, span], 7) == 7, 0.0, 1.0
                )


def build_edges(science, masks):
    visits, strip_rows, col_total = science.shape
    block = (visits, 8, col_total)
    top = pl.BlockSpec(block, lambda i: (0, 0, 0))
    bottom = pl.BlockSpec(block, lambda i: (0, strip_rows // 8 - 1, 0))
    edge = jax.ShapeDtypeStruct((col_total // CHUNK * visits * 2 * DHALF, CHUNK), F32)
    return pl.pallas_call(
        pack_edges,
        grid=(1,),
        out_shape=[edge, edge],
        in_specs=[top, bottom, top, bottom],
        out_specs=[whole(edge), whole(edge)],
        compiler_params=pltpu.CompilerParams(vmem_limit_bytes=VMEM_LIMIT),
        cost_estimate=pl.CostEstimate(flops=10**6, bytes_accessed=2 * 2**20, transcendentals=0),
    )(science, science, masks, masks)


def build_weights(visits, strip_rows, meta, widths, orders, coefficients, decor_kernel):
    scalar = pl.BlockSpec(memory_space=pltpu.SMEM)
    return pl.pallas_call(
        functools.partial(prepare, strip_rows),
        out_shape=[
            jax.ShapeDtypeStruct((4 * LANES, NFILT * LANES), BF16),
            jax.ShapeDtypeStruct((2, 2 * MROWS, NFILT * KWIN), BF16),
            jax.ShapeDtypeStruct((visits, GROUPS * strip_rows, SHIFTS * 2 * LANES), BF16),
            jax.ShapeDtypeStruct((8, LANES), F32),
        ],
        in_specs=[scalar] * 5,
        compiler_params=pltpu.CompilerParams(vmem_limit_bytes=VMEM_LIMIT),
        cost_estimate=pl.CostEstimate(flops=10**9, bytes_accessed=8 * 2**20, transcendentals=0),
    )(meta, widths, orders, coefficients, decor_kernel)


def whole(array):
    return pl.BlockSpec(array.shape, lambda i: (0,) * len(array.shape))


def fused(meta, back, token, templates, weights, science, masks, halo_up, halo_down):
    visits, strip_rows, col_total = science.shape
    return pl.pallas_call(
        body,
        out_shape=jax.ShapeDtypeStruct(science.shape, F32),
        in_specs=[pl.BlockSpec(memory_space=pltpu.SMEM)] * 2
        + [pl.BlockSpec(memory_space=pl.ANY)]
        + [pl.BlockSpec(memory_space=pltpu.VMEM)] * 2
        + [pl.BlockSpec(memory_space=pl.ANY)] * 3
        + [pl.BlockSpec(memory_space=pltpu.VMEM)]
        + [pl.BlockSpec(memory_space=pl.ANY)]
        + [pl.BlockSpec(memory_space=pltpu.VMEM)] * 2,
        out_specs=pl.BlockSpec(memory_space=pl.ANY),
        scratch_shapes=[
            pltpu.VMEM((2, NFILT * TROWS, CHUNK), BF16),
            pltpu.VMEM((2, NFILT * TROWS, CHUNK), BF16),
            pltpu.VMEM((visits, DROWS, col_total + LANES), F32),
            pltpu.VMEM((visits, strip_rows, col_total), F32),
            *[pltpu.VMEM(array.shape, array.dtype) for array in (*weights, masks)],
            pltpu.SemaphoreType.DMA((col_total // CHUNK,)),
            pltpu.SemaphoreType.DMA((4,)),
        ],
        compiler_params=pltpu.CompilerParams(vmem_limit_bytes=VMEM_LIMIT),
        cost_estimate=pl.CostEstimate(
            flops=14 * 10**9, bytes_accessed=10 * 2**20, transcendentals=0
        ),
    )(meta, back, token, *templates, *weights, science, masks, halo_up, halo_down)


def shards(
    science, template, gauss_widths, coeff_orders, coefficients, back_coeffs, masks, decor_kernel
):
    visits, strip_rows, col_total = science.shape
    strips = lax.axis_size("strip")
    strip = lax.axis_index("strip")
    core = lax.axis_index("visit") % 2
    up = [(i, i + 1) for i in range(strips - 1)]
    down = [(i + 1, i) for i in range(strips - 1)]

    size = lax.axis_size("visit")
    groups = [[i for i in range(size) if i % 2 == c] for c in range(2)]
    chips = size // 2
    above = lax.ppermute(template[strip_rows - 16 :], "strip", up)
    below = lax.ppermute(template[:16], "strip", down)
    edge_top, edge_bottom = build_edges(science, masks)
    above, below, edge_top, edge_bottom = lax.optimization_barrier(
        (above, below, edge_top, edge_bottom)
    )
    rimmed = jnp.concatenate([above, template, below], axis=0)
    copies = jnp.broadcast_to(rimmed[None], (chips,) + rimmed.shape)
    small = (copies, edge_top, edge_bottom, gauss_widths, coeff_orders, coefficients, decor_kernel)
    copies, edge_top, edge_bottom, *parameters = lax.optimization_barrier(small)
    own = lax.all_to_all(copies, "visit", 0, 0, axis_index_groups=groups)
    halo_up = lax.ppermute(edge_bottom, "strip", up)
    halo_down = lax.ppermute(edge_top, "strip", down)
    meta = jnp.stack([strip, core, strip_rows * strips]).astype(jnp.int32)
    *weights, token = build_weights(visits, strip_rows, meta, *parameters)
    own, token, halo_up, halo_down = lax.optimization_barrier((own, token, halo_up, halo_down))
    other = lax.ppermute(own, "visit", [(i, i ^ 1) for i in range(size)])
    return fused(meta, back_coeffs, token, (own, other), weights, science, masks, halo_up, halo_down)


def solution(mesh):
    return jax.shard_map(
        shards,
        mesh=mesh,
        in_specs=(
            P("visit", "strip", None),
            P("strip", "visit"),
            P(),
            P(),
            P("visit", None, None),
            P("visit", None),
            P("visit", "strip", None),
            P("visit", None, None),
        ),
        out_specs=P("visit", "strip", None),
        check_vma=False,
    )
```

```python
import functools

import jax
import jax.numpy as jnp
from jax import lax
from jax.experimental import pallas as pl
from jax.experimental.pallas import tpu as pltpu
from jax.sharding import PartitionSpec as P

KSIZE = 21
NBASIS = 21
NFILT = 8
NPOLY = 6
DKSIZE = 11
KHALF = 10
DHALF = 5
LANES = 128
CHUNK = 512
SHIFTS = 4
GROUPS = 3
VMEM_LIMIT = 56 * 1024 * 1024
TROWS = 96
HALFROWS = 40
MROWS = 6 * HALFROWS
KWIN = 64
DROWS = 80
F32 = jnp.float32
BF16 = jnp.bfloat16


def basis_pairs():
    basis_list = []
    for family_base, degree in ((0, 4), (5, 2)):
        for exponent in range(degree + 1):
            for second in range(degree + 1 - exponent):
                basis_list.append((family_base + exponent, family_base + second))
    return basis_list


def split(x):
    high = x.astype(BF16)
    return high, (x - high.astype(F32)).astype(BF16)


def strip_rows_norm(meta, half, strip_rows):
    rows = lax.broadcasted_iota(jnp.int32, (HALFROWS, LANES), 0) + (
        meta[0] * strip_rows - 8 + half * HALFROWS
    )
    return (2.0 * rows.astype(F32) + 1.0) / meta[2].astype(F32) - 1.0


def family_filters(widths, position):
    offsets = lax.broadcasted_iota(jnp.int32, (1, LANES), 1) - LANES // 2
    rows = []
    for family, degree in ((0, 4), (1, 2)):
        spread = 0.75 * widths[family].astype(F32)

        def profile(at):
            real = at.astype(F32)
            return jnp.where(
                jnp.abs(at) <= KHALF, jnp.exp(-(real * real) / (2.0 * spread * spread)), 0.0
            )

        current = profile(position) / jnp.sum(profile(offsets), axis=1, keepdims=True)
        scaled = position.astype(F32) / spread
        for exponent in range(degree + 1):
            rows.append(current)
            current = current * scaled
    return rows


def prepare(
    strip_rows,
    meta,
    widths,
    orders,
    coefficients,
    decor_kernel,
    weights,
):
    visits = coefficients.shape[0]
    col_weights = weights.at[: 4 * LANES]
    row_weights = weights.at[4 * LANES : 4 * LANES + 2 * MROWS]
    decor_weights = weights.at[4 * LANES + 2 * MROWS :]
    lane_row = lax.broadcasted_iota(jnp.int32, (1, LANES), 1)
    filters = family_filters(widths, jnp.where(lane_row < LANES // 2, lane_row, lane_row - LANES))
    place = jnp.where(lane_row >= LANES - 2, lane_row - LANES, lane_row) + 2
    odd_place = place >= KWIN
    inner = jnp.where(odd_place, place - KWIN, place)
    windows = family_filters(widths, KHALF - inner)
    degrees = (0, 1, 1, 2, 2, 2)
    taps = {}
    for s in range(visits):
        for t in range(NPOLY):
            sums = [None] * NFILT
            for k, (row_kernel, col_kernel) in enumerate(basis_pairs()):
                weight = jnp.where(orders[k] >= degrees[t], coefficients[s, k, t], 0.0)
                term = weight * windows[row_kernel]
                sums[col_kernel] = term if sums[col_kernel] is None else sums[col_kernel] + term
            for tile in range(NFILT // 2):
                taps[s, t, tile] = jnp.where(odd_place, sums[2 * tile + 1], sums[2 * tile])
    source = lax.broadcasted_iota(jnp.int32, (LANES, LANES), 0)
    target = lax.broadcasted_iota(jnp.int32, (LANES, LANES), 1)
    near = jnp.abs(target - source) <= KHALF
    for j in range(NFILT):
        lanes = slice(j * LANES, (j + 1) * LANES)
        flat = jnp.broadcast_to(filters[j], (LANES, LANES))
        ring = pltpu.roll(flat, 0, 1, stride=1, stride_axis=0)
        high = ring.astype(BF16).astype(F32)
        low = ring - high
        col_weights[:LANES, lanes] = jnp.where(near, high, 0.0).astype(BF16)
        col_weights[LANES : 2 * LANES, lanes] = jnp.where(near, high, 0.0).astype(BF16)
        col_weights[2 * LANES : 3 * LANES, lanes] = jnp.where(near, low, 0.0).astype(BF16)
        side_high = jnp.where(near, 0.0, high)
        side_low = jnp.where(near, 0.0, low)
        packed = side_high + pltpu.roll(side_high, 20, 0) + pltpu.roll(side_low, 40, 0)
        col_weights[3 * LANES :, lanes] = packed.astype(BF16)
    for half in range(2):
        yn = strip_rows_norm(meta, half, strip_rows)
        for tile in range(4):
            parts = []
            for s in range(visits):
                rolled = []
                for t in range(NPOLY):
                    flat = jnp.broadcast_to(taps[s, t, tile], (HALFROWS, LANES))
                    rolled.append(pltpu.roll(flat, 8 * half, 1, stride=1, stride_axis=0))
                parts.append(rolled[0] + yn * (rolled[2] + yn * rolled[5]))
                parts.append(rolled[1] + yn * rolled[4])
                parts.append(rolled[3])
            high, low = split(jnp.concatenate(parts, axis=0))
            first = half * NFILT * KWIN + tile * LANES
            row_weights[:MROWS, first : first + LANES] = high
            row_weights[MROWS:, first : first + LANES] = low
    for s in range(visits):
        for slot in range(SHIFTS * GROUPS):
            group, shift = slot // SHIFTS, slot % SHIFTS
            first = (s * GROUPS + group) * strip_rows
            rows = slice(first, first + strip_rows)
            lanes = slice(shift * 2 * LANES, (shift + 1) * 2 * LANES)
            if slot < DKSIZE:
                base = jnp.zeros((1, LANES), F32)
                for tap in range(DKSIZE):
                    base = jnp.where(lane_row == DKSIZE - 1 - tap, decor_kernel[s, tap, slot], base)
                high = base.astype(BF16).astype(F32)
                low = base - high
                wide = jnp.concatenate(
                    [high + pltpu.roll(high, DROWS, 1), pltpu.roll(low, 2 * DROWS - LANES, 1)], axis=1
                )
                flat = jnp.broadcast_to(wide, (strip_rows, 2 * LANES))
                turned = pltpu.roll(flat, 3, 1, stride=1, stride_axis=0).astype(BF16)
            else:
                turned = jnp.zeros((strip_rows, 2 * LANES), BF16)
            decor_weights[rows, lanes] = turned


def body(
    meta,
    back,
    own,
    other,
    weights,
    science,
    masks,
    halo_up,
    halo_down,
    out,
    high_filtered,
    low_filtered,
    diffs,
    staged,
    sent,
):
    core = meta[1]
    visits, strip_rows, col_total = science.shape
    steps = col_total // CHUNK
    chips = CHUNK // 512
    blocks_here = 4 * chips
    diffs[:, :, col_total:] = jnp.zeros((visits, DROWS, LANES), F32)
    lane = lax.broadcasted_iota(jnp.int32, (TROWS, LANES), 1)
    edge_lane = lax.broadcasted_iota(jnp.int32, (strip_rows, LANES), 1)
    low_lanes, high_lanes = slice(0, LANES), slice(LANES, 2 * LANES)

    def strip_of(chip, odd, lanes):
        return jnp.where(core == odd, own[chip, :, lanes], other[chip, :, lanes])

    def differences(step):
        slot = step % 2
        first_chip = step * chips
        last_chip = first_chip + chips
        empty = jnp.zeros((TROWS, LANES), F32)
        blocks = [strip_of(first_chip - 1, 1, high_lanes) if step else empty]
        for chip in range(first_chip, last_chip):
            for odd in range(2):
                blocks.append(strip_of(chip, odd, low_lanes))
                blocks.append(strip_of(chip, odd, high_lanes))
        blocks.append(strip_of(last_chip, 0, low_lanes) if step < steps - 1 else empty)
        stacked = []
        for b in range(blocks_here):
            high, low = split(blocks[b + 1])
            side = jnp.where(
                lane < KHALF, blocks[b + 2], jnp.where(lane >= LANES - KHALF, blocks[b], 0.0)
            )
            side_high = side.astype(BF16).astype(F32)
            side_low = side - side_high
            packed = side_high + pltpu.roll(side_low, 20, 1) + pltpu.roll(side_high, 40, 1)
            stacked.append(jnp.concatenate([high, low, high, packed.astype(BF16)], axis=1))
        lhs = jnp.concatenate(stacked, axis=0)
        for pair in range(4):
            filtered = jnp.dot(
                lhs, weights[: 4 * LANES, 256 * pair : 256 * (pair + 1)], preferred_element_type=F32
            )
            for inner in range(2):
                first = (2 * pair + inner) * TROWS
                for b in range(blocks_here):
                    high, low = split(
                        filtered[TROWS * b : TROWS * (b + 1), LANES * inner : LANES * (inner + 1)]
                    )
                    high_filtered[slot, first : first + TROWS, LANES * b : LANES * (b + 1)] = high
                    low_filtered[slot, first : first + TROWS, LANES * b : LANES * (b + 1)] = low

        columns = lax.broadcasted_iota(jnp.int32, (8, CHUNK), 1) + step * CHUNK
        xn = (2.0 * columns.astype(F32) + 1.0) / float(steps * CHUNK) - 1.0
        xn = jnp.concatenate([xn] * (HALFROWS // 8), axis=0)
        start = step * CHUNK
        span = slice(start, start + CHUNK)
        for half in range(2):
            starts = [j * TROWS + 32 * half for j in range(NFILT)]
            rhs_high = [high_filtered[slot, r : r + KWIN, :] for r in starts]
            rhs_low = [low_filtered[slot, r : r + KWIN, :] for r in starts]
            row_first = 4 * LANES
            row_lanes = slice(half * NFILT * KWIN, (half + 1) * NFILT * KWIN)
            wide = jnp.dot(
                weights[row_first : row_first + 2 * MROWS, row_lanes], jnp.concatenate(rhs_high, axis=0), preferred_element_type=F32
            )
            rest = jnp.dot(
                weights[row_first : row_first + MROWS, row_lanes], jnp.concatenate(rhs_low, axis=0), preferred_element_type=F32
            )
            summed = wide[:MROWS] + wide[MROWS:] + rest
            yn = strip_rows_norm(meta, half, strip_rows)[:, :1]
            for s in range(visits):
                base = s * 3 * HALFROWS
                back0 = back[s, 0] + yn * (back[s, 2] + yn * back[s, 5])
                back1 = back[s, 1] + yn * back[s, 4]
                g0 = summed[base : base + HALFROWS] + back0
                g1 = summed[base + HALFROWS : base + 2 * HALFROWS] + back1
                g2 = summed[base + 2 * HALFROWS : base + 3 * HALFROWS] + back[s, 3]
                model = g0 + xn * (g1 + xn * g2)
                rows = slice(32 * half, 32 * half + 32)
                fine = jnp.where(jnp.bitwise_and(masks[s, rows, span], 7) == 7, 0.0, 1.0)
                data, good = science[s, rows, span], fine
                blank = jnp.zeros((8 - DHALF, CHUNK), F32)
                first = (step * visits + s) * 2 * DHALF
                halo = halo_down if half else halo_up
                halo_data = halo[first : first + DHALF]
                halo_good = halo[first + DHALF : first + 2 * DHALF]
                if half == 0:
                    data = jnp.concatenate([blank, halo_data, data], axis=0)
                    good = jnp.concatenate([blank, halo_good, good], axis=0)
                else:
                    data = jnp.concatenate([data, halo_data, blank], axis=0)
                    good = jnp.concatenate([good, halo_good, blank], axis=0)
                diffs[s, half * HALFROWS : (half + 1) * HALFROWS, span] = jnp.where(
                    good > 0.5, data - model, 0.0
                )

    def shifted_products(s, window, width):
        parts = []
        for shift in range(SHIFTS):
            turned = pltpu.roll(window, width + LANES - DHALF + shift, 1)[:, :width]
            high, low = split(turned)
            parts += [high, low, high, jnp.zeros((16, width), BF16)]
        first = 4 * LANES + 2 * MROWS + s * GROUPS * strip_rows
        return jnp.dot(
            weights[first : first + GROUPS * strip_rows], jnp.concatenate(parts, axis=0), preferred_element_type=F32
        )

    def left_of_patch(s):
        window = jnp.concatenate([jnp.zeros((DROWS, LANES), F32), diffs[s, :, :LANES]], axis=1)
        product = shifted_products(s, window, LANES)
        start_carry = jnp.zeros((strip_rows, LANES), F32)
        for group in range(1, GROUPS):
            shift = SHIFTS * group
            turned = pltpu.roll(product[group * strip_rows : (group + 1) * strip_rows], shift, 1)
            start_carry = start_carry + jnp.where(edge_lane < shift, turned, 0.0)
        return start_carry

    def decorrelate(step, carries):
        start = step * CHUNK
        spilled = []
        for s in range(visits):
            product = shifted_products(s, diffs[s, :, start : start + CHUNK + LANES], CHUNK)
            total = product[:strip_rows]
            to_right = jnp.zeros((strip_rows, LANES), F32)
            for group in range(1, GROUPS):
                shift = SHIFTS * group
                turned = pltpu.roll(product[group * strip_rows : (group + 1) * strip_rows], shift, 1)
                first = turned[:, :LANES]
                to_right = to_right + jnp.where(edge_lane < shift, first, 0.0)
                first = jnp.where(edge_lane < shift, 0.0, first)
                total = total + jnp.concatenate([first, turned[:, LANES:]], axis=1)
            staged[s, :, start : start + LANES] = total[:, :LANES] + carries[s]
            staged[s, :, start + LANES : start + CHUNK] = total[:, LANES:]
            spilled.append(to_right)
        return spilled

    def send(step):
        span = pl.ds(step * CHUNK, CHUNK)
        return pltpu.make_async_copy(
            staged.at[:, :, span], out.at[:, :, span], sent.at[step]
        )

    for step in range(steps):
        differences(step)
    carries = [left_of_patch(s) for s in range(visits)]
    for step in range(steps):
        carries = decorrelate(step, carries)
        send(step).start()
    for step in range(steps):
        send(step).wait()


def pack_edges(science_top, science_bottom, masks_top, masks_bottom, edge_top, edge_bottom):
    for data, bits, edge, begin in (
        (science_top, masks_top, edge_top, 0),
        (science_bottom, masks_bottom, edge_bottom, 8 - DHALF),
    ):
        rows = slice(begin, begin + DHALF)
        for s in range(data.shape[0]):
            for chunk in range(data.shape[2] // CHUNK):
                span = slice(chunk * CHUNK, (chunk + 1) * CHUNK)
                first = (chunk * data.shape[0] + s) * 2 * DHALF
                edge[first : first + DHALF] = data[s, rows, span]
                edge[first + DHALF : first + 2 * DHALF] = jnp.where(
                    jnp.bitwise_and(bits[s, rows, span], 7) == 7, 0.0, 1.0
                )


def build_edges(science, masks):
    visits, strip_rows, col_total = science.shape
    block = (visits, 8, col_total)
    top = pl.BlockSpec(block, lambda i: (0, 0, 0))
    bottom = pl.BlockSpec(block, lambda i: (0, strip_rows // 8 - 1, 0))
    edge = jax.ShapeDtypeStruct((col_total // CHUNK * visits * 2 * DHALF, CHUNK), F32)
    return pl.pallas_call(
        pack_edges,
        grid=(1,),
        out_shape=[edge, edge],
        in_specs=[top, bottom, top, bottom],
        out_specs=[whole(edge), whole(edge)],
        compiler_params=pltpu.CompilerParams(vmem_limit_bytes=VMEM_LIMIT),
        cost_estimate=pl.CostEstimate(flops=10**6, bytes_accessed=2 * 2**20, transcendentals=0),
    )(science, science, masks, masks)


def build_weights(visits, strip_rows, meta, widths, orders, coefficients, decor_kernel):
    scalar = pl.BlockSpec(memory_space=pltpu.SMEM)
    return pl.pallas_call(
        functools.partial(prepare, strip_rows),
        out_shape=jax.ShapeDtypeStruct(
            (4 * LANES + 2 * MROWS + visits * GROUPS * strip_rows, NFILT * LANES), BF16
        ),
        in_specs=[scalar] * 5,
        compiler_params=pltpu.CompilerParams(vmem_limit_bytes=VMEM_LIMIT),
        cost_estimate=pl.CostEstimate(flops=10**9, bytes_accessed=8 * 2**20, transcendentals=0),
    )(meta, widths, orders, coefficients, decor_kernel)


def whole(array):
    return pl.BlockSpec(array.shape, lambda i: (0,) * len(array.shape))


def fused(meta, back, templates, weights, science, masks, halo_up, halo_down):
    visits, strip_rows, col_total = science.shape
    return pl.pallas_call(
        body,
        out_shape=jax.ShapeDtypeStruct(science.shape, F32),
        in_specs=[pl.BlockSpec(memory_space=pltpu.SMEM)] * 2
        + [pl.BlockSpec(memory_space=pltpu.VMEM)] * 7,
        out_specs=pl.BlockSpec(memory_space=pl.ANY),
        scratch_shapes=[
            pltpu.VMEM((2, NFILT * TROWS, CHUNK), BF16),
            pltpu.VMEM((2, NFILT * TROWS, CHUNK), BF16),
            pltpu.VMEM((visits, DROWS, col_total + LANES), F32),
            pltpu.VMEM((visits, strip_rows, col_total), F32),
            pltpu.SemaphoreType.DMA((col_total // CHUNK,)),
        ],
        compiler_params=pltpu.CompilerParams(vmem_limit_bytes=20 * 1024 * 1024),
        cost_estimate=pl.CostEstimate(
            flops=14 * 10**9, bytes_accessed=10 * 2**20, transcendentals=0
        ),
    )(meta, back, *templates, weights, science, masks, halo_up, halo_down)


def shards(
    science, template, gauss_widths, coeff_orders, coefficients, back_coeffs, masks, decor_kernel
):
    visits, strip_rows, col_total = science.shape
    strips = lax.axis_size("strip")
    strip = lax.axis_index("strip")
    core = lax.axis_index("visit") % 2
    up = [(i, i + 1) for i in range(strips - 1)]
    down = [(i + 1, i) for i in range(strips - 1)]

    size = lax.axis_size("visit")
    groups = [[i for i in range(size) if i % 2 == c] for c in range(2)]
    chips = size // 2
    above = lax.ppermute(template[strip_rows - 16 :], "strip", up)
    below = lax.ppermute(template[:16], "strip", down)
    edge_top, edge_bottom = build_edges(science, masks)
    above, below, edge_top, edge_bottom = lax.optimization_barrier(
        (above, below, edge_top, edge_bottom)
    )
    rimmed = jnp.concatenate([above, template, below], axis=0)
    copies = jnp.broadcast_to(rimmed[None], (chips,) + rimmed.shape)
    small = (copies, edge_top, edge_bottom, gauss_widths, coeff_orders, coefficients, decor_kernel)
    copies, edge_top, edge_bottom, *parameters = lax.optimization_barrier(small)
    own = lax.all_to_all(copies, "visit", 0, 0, axis_index_groups=groups)
    halo_up = lax.ppermute(edge_bottom, "strip", up)
    halo_down = lax.ppermute(edge_top, "strip", down)
    meta = jnp.stack([strip, core, strip_rows * strips]).astype(jnp.int32)
    weights = build_weights(visits, strip_rows, meta, *parameters)
    own, weights, halo_up, halo_down = lax.optimization_barrier((own, weights, halo_up, halo_down))
    other = lax.ppermute(own, "visit", [(i, i ^ 1) for i in range(size)])
    return fused(meta, back_coeffs, (own, other), weights, science, masks, halo_up, halo_down)


def solution(mesh):
    return jax.shard_map(
        shards,
        mesh=mesh,
        in_specs=(
            P("visit", "strip", None),
            P("strip", "visit"),
            P(),
            P(),
            P("visit", None, None),
            P("visit", None),
            P("visit", "strip", None),
            P("visit", None, None),
        ),
        out_specs=P("visit", "strip", None),
        check_vma=False,
    )
```
